512 devices in a mesh: grp: 8 (over x, core), col: 64 (over z, y).
Axes of the slice: x: 4, y: 8, z: 8, core: 2. Of those that a mesh axis runs over, the one named last changes fastest.
Arguments:
- panel_blocks: bfloat16 [1024, 128, 128], P(('grp', 'col')), may hold values from -6 to 6
- panel_rows: int32 [1024], P(('grp', 'col')), may hold values from 0 to 7, as said below
- panel_inner: int32 [1024], P(('grp', 'col')), may hold values from 0 to 63, as said below
- right_blocks: bfloat16 [64, 256, 128, 128], P('grp', 'col'), may hold values from -0.1875 to 0.1875
- right_columns: int32 [64, 256], P('grp', 'col'), may hold values from 0 to 7, as said below
Outputs:
- product: bfloat16 [8192, 65536], P('grp', 'col')
The draws below stay inside these ranges and needn't reach their ends.
Inputs may be any that keep to these rules, and one draw needn't show every extreme that they name: Within one group the pairs (panel_rows, panel_inner) are distinct, and every block row of a group has exactly 16 blocks. Within one group the pairs (panel_rows, panel_inner) are distinct. `right_columns`: the 4 block columns listed for one block row and one column set are distinct.
All inputs are finite; a program needn't handle non-finite values.
Results may differ from the reference program's by a relative error of at most 0.001.
Values may be sent and summed in bfloat16 or wider, within the bound.
No kernel may reach another device: no remote copies, remote signals or barrier semaphores. Data moves between devices by JAX's collectives and lax.ppermute only.
A program may use at most 128 MiB of HBM per device.

```python
import math
import jax
import jax.numpy as jnp
from jax import lax

BS = 128
NA_DEV = 2
RG = 8
KS = 64
JB = 8
NBR = 4
PER_ROW = 16
N_GRP = 8
N_COL = 64


def panel_pairs(key):
    span = NA_DEV * N_COL
    per_row = span // RG
    first = jax.random.fold_in(key, 11)
    second = jax.random.fold_in(key, 12)
    scores = jax.random.randint(first, (N_GRP, RG, KS), 0, 2 ** 20) * KS + lax.broadcasted_iota(jnp.int32, (N_GRP, RG, KS), 2)
    unused, chosen = lax.top_k(scores, per_row)
    inner_ids = chosen.reshape(N_GRP, span).astype(jnp.int32)
    row_ids = lax.broadcasted_iota(jnp.int32, (N_GRP, RG, per_row), 1).reshape(N_GRP, span)
    order_keys = jax.random.randint(second, (N_GRP, span), 0, 2 ** 20) * span + lax.broadcasted_iota(jnp.int32, (N_GRP, span), 1)
    order = jnp.argsort(order_keys, axis=1, stable=True)
    row_ids = jnp.take_along_axis(row_ids, order, axis=1)
    inner_ids = jnp.take_along_axis(inner_ids, order, axis=1)
    return (row_ids.reshape(-1), inner_ids.reshape(-1))


def draw_panel_rows(key, part):
    row_ids, inner_ids = panel_pairs(key)
    return row_ids


def draw_panel_inner(key, part):
    row_ids, inner_ids = panel_pairs(key)
    return inner_ids


def draw_right_columns(key, part):
    key = jax.random.fold_in(key, 7)
    scores = jax.random.randint(key, (KS, N_COL, JB), 0, 2 ** 20) * JB + lax.broadcasted_iota(jnp.int32, (KS, N_COL, JB), 2)
    unused, chosen = lax.top_k(scores, NBR)
    return chosen.reshape(KS, N_COL * NBR).astype(jnp.int32)


def levels(key, extent, split, smallest, high):
    level = 1.0
    for dim, blocks in split:
        steps = jax.random.uniform(jax.random.fold_in(jax.random.fold_in(key, 6), dim), (blocks,), jnp.float32, smallest / len(split), high / len(split))
        level = level * jnp.repeat(jnp.exp(steps), extent[dim] // blocks).reshape((-1,) + (1,) * (len(extent) - 1 - dim))
    return level


def bell_draw(rng, dims, spread, most, split=(), kind=jnp.bfloat16):
    values = jax.random.normal(rng, dims, jnp.float32) * spread
    if len(split) > 0:
        values = levels(rng, dims, split, -0.22, 0.18) * values
    return jnp.clip(values, min=-most, max=most).astype(kind)


def setup_inputs(seed: int = 0) -> dict:
    arg_keys = jax.random.split(jax.random.key(seed), 6)
    return {
        "panel_blocks": bell_draw(arg_keys[0], (N_GRP * N_COL * NA_DEV, BS, BS), 1.0, 6.0, ((0, 512),)),
        "panel_rows": draw_panel_rows(jax.random.fold_in(arg_keys[5], 71), 0),
        "panel_inner": draw_panel_inner(jax.random.fold_in(arg_keys[5], 71), 0),
        "right_blocks": bell_draw(arg_keys[3], (KS, N_COL * NBR, BS, BS), (BS * max(1, PER_ROW * NBR // JB)) ** -0.5, 0.1875, ((0, 8), (1, 64))),
        "right_columns": draw_right_columns(jax.random.fold_in(arg_keys[5], 71), 0),
    }


def accumulate(running, blocks, row_ids, inner_ids, section_blocks, section_columns):
    chosen = section_blocks[inner_ids]
    products = jnp.einsum("nij,nmjk->nmik", blocks.astype(jnp.float32), chosen.astype(jnp.float32), preferred_element_type=jnp.float32)
    targets = row_ids[:, None] * JB + section_columns[inner_ids]
    return running.at[targets.reshape(-1)].add(products.reshape(-1, BS, BS))


def panel_product(blocks, row_ids, inner_ids, section_blocks, section_columns):
    count = blocks.shape[0]
    step = math.gcd(count, 16)
    grouped = (blocks.reshape(count // step, step, BS, BS), row_ids.reshape(count // step, step), inner_ids.reshape(count // step, step))

    def advance(running, pieces):
        return accumulate(running, pieces[0], pieces[1], pieces[2], section_blocks, section_columns), None

    start = jnp.zeros((RG * JB, BS, BS), jnp.float32)
    running, unused = lax.scan(advance, start, grouped)
    dense = running.reshape(RG, JB, BS, BS).transpose(0, 2, 1, 3).reshape(RG * BS, JB * BS)
    return dense.astype(jnp.bfloat16)


def reference(panel_blocks, panel_rows, panel_inner, right_blocks, right_columns):
    span = NA_DEV * N_COL
    group_blocks = panel_blocks.reshape(N_GRP, span, BS, BS)
    group_rows = panel_rows.reshape(N_GRP, span)
    group_inner = panel_inner.reshape(N_GRP, span)
    set_blocks = right_blocks.reshape(KS, N_COL, NBR, BS, BS).transpose(1, 0, 2, 3, 4)
    set_columns = right_columns.reshape(KS, N_COL, NBR).transpose(1, 0, 2)

    def per_group(group):
        def per_set(column_set):
            return panel_product(group[0], group[1], group[2], column_set[0], column_set[1])
        return lax.map(per_set, (set_blocks, set_columns))

    result = lax.map(per_group, (group_blocks, group_rows, group_inner))
    return result.transpose(0, 2, 1, 3).reshape(N_GRP * RG * BS, N_COL * JB * BS)
```

```python
import jax
import jax.numpy as jnp
from jax import lax
from jax.experimental import pallas as pl
from jax.experimental.pallas import tpu as pltpu
from jax.sharding import PartitionSpec as P

BS = 128
RG = 8
KS = 64
JB = 8
NBR = 4
PER_ROW = 16
N_X = 4
N_Y = 8
N_Z = 8
PAD = 16
OWN_K = 8
R_ROWS = OWN_K * NBR * BS
L_ROWS = 2 * BS
N_LEFT = 128
N_RIGHT = KS * NBR


def shift_x(step):
    return [(x * 2 + c, ((x + step) % N_X) * 2 + c) for x in range(N_X) for c in range(2)]


SWAP_CORES = [(g, g ^ 1) for g in range(2 * N_X)]
Y_LINES = [[z * N_Y + y for y in range(N_Y)] for z in range(N_Z)]
Z_LINES = [[z * N_Y + y for z in range(N_Z)] for y in range(N_Y)]


def multiply_kernel(place, columns, ids, left, *refs):
    pieces, (out, left_buf, right_buf, table, order, filled, sem) = refs[:10], refs[10:]
    row = pl.program_id(0)

    @pl.when(row == 0)
    def load():
        copies = [pltpu.make_async_copy(left, left_buf, sem.at[0])]
        slot = 0
        for i, piece in enumerate(pieces):
            rows = piece.shape[0]
            blocks = rows // BS
            copies.append(
                pltpu.make_async_copy(
                    piece.at[pl.ds(0, blocks * BS)],
                    right_buf.at[pl.ds(slot * BS, blocks * BS)],
                    sem.at[i + 1],
                )
            )
            slot += blocks
        for copy in copies:
            copy.start()
        right_buf[pl.ds(N_RIGHT * BS, BS), :] = jnp.zeros((BS, BS), jnp.bfloat16)
        own_x, own_core = place[0] // 2, place[0] % 2
        for r in range(RG):
            filled[r] = 0

        def list_row(i, carry):
            device, b = i // 2, i % 2
            r = ids[device * 4 + b]
            n = filled[r]
            order[(r * PER_ROW + n) * 2] = device * (L_ROWS + PAD) + b * BS
            order[(r * PER_ROW + n) * 2 + 1] = ids[device * 4 + 2 + b]
            filled[r] = n + 1
            return carry

        lax.fori_loop(0, N_LEFT, list_row, 0, unroll=4)

        def clear(i, carry):
            table[i] = N_RIGHT * BS
            return carry

        lax.fori_loop(0, KS * JB, clear, 0, unroll=16)

        def fill(k, carry):
            g = k // OWN_K
            s = ((g + own_core) % 2) * N_X + (g // 2 + N_X - own_x) % N_X
            first = (s * OWN_K + k % OWN_K) * NBR
            for m in range(NBR):
                table[k * JB + columns[first + m]] = (first + m) * BS
            return carry

        lax.fori_loop(0, KS, fill, 0, unroll=2)
        for copy in copies:
            copy.wait()

    starts = [pl.multiple_of(order[(row * PER_ROW + p) * 2], BS // 8) for p in range(PER_ROW)]
    inner = [order[(row * PER_ROW + p) * 2 + 1] * JB for p in range(PER_ROW)]
    lhs = jnp.concatenate([left_buf[pl.ds(s, BS), :] for s in starts], axis=1)
    for j in range(0, JB, 2):
        rhs = jnp.concatenate(
            [
                jnp.concatenate(
                    [right_buf[pl.ds(pl.multiple_of(table[k + j + h], BS), BS), :] for h in range(2)],
                    axis=1,
                )
                for k in inner
            ],
            axis=0,
        )
        out[:, j * BS : (j + 2) * BS] = jnp.dot(lhs, rhs, preferred_element_type=jnp.float32).astype(out.dtype)


def multiply(place, columns, ids, left, pieces):
    smem = pl.BlockSpec(memory_space=pltpu.SMEM)
    hbm = pl.BlockSpec(memory_space=pl.ANY)
    return pl.pallas_call(
        multiply_kernel,
        grid=(RG,),
        out_shape=jax.ShapeDtypeStruct((RG * BS, JB * BS), jnp.bfloat16),
        in_specs=[smem] * 3 + [hbm] * (1 + len(pieces)),
        out_specs=pl.BlockSpec((BS, JB * BS), lambda r: (r, 0)),
        scratch_shapes=[
            pltpu.VMEM(left.shape, jnp.bfloat16),
            pltpu.VMEM(((N_RIGHT + 1) * BS, BS), jnp.bfloat16),
            pltpu.SMEM((KS * JB,), jnp.int32),
            pltpu.SMEM((N_LEFT * 2,), jnp.int32),
            pltpu.SMEM((RG,), jnp.int32),
            pltpu.SemaphoreType.DMA((1 + len(pieces),)),
        ],
        compiler_params=pltpu.CompilerParams(vmem_limit_bytes=32 * 2**20),
        cost_estimate=pl.CostEstimate(flops=4 * 2**30, bytes_accessed=14 * 2**20, transcendentals=0),
    )(place, columns, ids, left, *pieces)


def tail(values):
    flat = values.astype(jnp.bfloat16).reshape(1, -1)
    return jnp.pad(flat, ((0, PAD - 1), (0, BS - flat.shape[1])))


def gather_right(own):
    after = lax.ppermute(own, "grp", shift_x(-1))
    before = lax.ppermute(own, "grp", shift_x(1))
    far_head = lax.ppermute(before[: R_ROWS // 2], "grp", shift_x(1))
    far_tail = lax.ppermute(after[R_ROWS // 2 :], "grp", shift_x(-1))
    mine = [own, after, far_head, far_tail, before]
    return mine + [lax.ppermute(v, "grp", SWAP_CORES) for v in mine]


def gather_left(own):
    copies = jnp.broadcast_to(own[None], (N_Y,) + own.shape)
    line = lax.all_to_all(copies, "col", 0, 0, axis_index_groups=Y_LINES)
    return lax.all_gather(line, "col", axis=0, tiled=True, axis_index_groups=Z_LINES)


def body(panel_blocks, panel_rows, panel_inner, right_blocks, right_columns):
    right = jnp.concatenate([right_blocks.reshape(R_ROWS, BS), tail(right_columns)])
    left = jnp.concatenate(
        [panel_blocks.reshape(L_ROWS, BS), tail(jnp.concatenate([panel_rows, panel_inner]))]
    )
    pieces = gather_right(right)
    lefts = gather_left(left)
    columns = jnp.concatenate(
        [v[-PAD, : OWN_K * NBR] for v in pieces if v.shape[0] % BS == PAD]
    ).astype(jnp.int32)
    ids = lefts[:, L_ROWS, :4].astype(jnp.int32).reshape(-1)
    place = lax.axis_index("grp").reshape(1)
    return multiply(place, columns, ids, lefts.reshape(-1, BS), pieces)


def solution(mesh):
    placed = (
        P(("grp", "col"), None, None),
        P(("grp", "col")),
        P(("grp", "col")),
        P("grp", "col", None, None),
        P("grp", "col"),
    )
    return jax.shard_map(
        body, mesh=mesh, in_specs=placed, out_specs=P("grp", "col"), check_vma=False
    )
```

```python
import jax
import jax.numpy as jnp
from jax import lax
from jax.experimental import pallas as pl
from jax.experimental.pallas import tpu as pltpu
from jax.sharding import PartitionSpec as P

BS = 128
RG = 8
KS = 64
JB = 8
NBR = 4
PER_ROW = 16
N_X = 4
N_Y = 8
N_Z = 8
PAD = 16
OWN_K = 8
R_ROWS = OWN_K * NBR * BS
L_ROWS = 2 * BS
N_LEFT = 128
N_RIGHT = KS * NBR


def shift_x(step):
    return [(x * 2 + c, ((x + step) % N_X) * 2 + c) for x in range(N_X) for c in range(2)]


SWAP_CORES = [(g, g ^ 1) for g in range(2 * N_X)]
Y_LINES = [[z * N_Y + y for y in range(N_Y)] for z in range(N_Z)]
Z_LINES = [[z * N_Y + y for z in range(N_Z)] for y in range(N_Y)]


def arrange_kernel(place, columns, ids, *refs):
    pieces, (right, order, found, table, filled, sem) = refs[:10], refs[10:]
    copies = []
    slot = 0
    for i, piece in enumerate(pieces):
        blocks = piece.shape[0] // BS
        copies.append(
            pltpu.make_async_copy(
                piece.at[pl.ds(0, blocks * BS)], right.at[pl.ds(slot * BS, blocks * BS)], sem.at[i]
            )
        )
        slot += blocks
    for copy in copies:
        copy.start()
    right[pl.ds(N_RIGHT * BS, BS), :] = jnp.zeros((BS, BS), jnp.bfloat16)
    own_x, own_core = place[0] // 2, place[0] % 2

    def clear(i, carry):
        table[i] = N_RIGHT * BS
        return carry

    lax.fori_loop(0, KS * JB, clear, 0, unroll=16)

    def fill(k, carry):
        g = k // OWN_K
        s = ((g + own_core) % 2) * N_X + (g // 2 + N_X - own_x) % N_X
        first = (s * OWN_K + k % OWN_K) * NBR
        for m in range(NBR):
            table[k * JB + columns[first + m]] = (first + m) * BS
        return carry

    lax.fori_loop(0, KS, fill, 0, unroll=2)
    for r in range(RG):
        filled[r] = 0

    def list_row(i, carry):
        device, b = i // 2, i % 2
        r = ids[device * 4 + b]
        k = ids[device * 4 + 2 + b]
        n = filled[r]
        p = r * PER_ROW + n
        order[p] = i * BS
        for j in range(JB):
            found[p * JB + j] = table[k * JB + j]
        filled[r] = n + 1
        return carry

    lax.fori_loop(0, N_LEFT, list_row, 0, unroll=2)
    for copy in copies:
        copy.wait()


def arrange(place, columns, ids, pieces):
    smem = pl.BlockSpec(memory_space=pltpu.SMEM)
    return pl.pallas_call(
        arrange_kernel,
        out_shape=(
            pltpu.VMEM(((N_RIGHT + 1) * BS, BS), jnp.bfloat16),
            jax.ShapeDtypeStruct((N_LEFT,), jnp.int32),
            jax.ShapeDtypeStruct((N_LEFT * JB,), jnp.int32),
        ),
        in_specs=[smem] * 3 + [pl.BlockSpec(memory_space=pl.ANY)] * len(pieces),
        out_specs=(pl.BlockSpec(memory_space=pltpu.VMEM), smem, smem),
        scratch_shapes=[
            pltpu.SMEM((KS * JB,), jnp.int32),
            pltpu.SMEM((RG,), jnp.int32),
            pltpu.SemaphoreType.DMA((len(pieces),)),
        ],
        compiler_params=pltpu.CompilerParams(vmem_limit_bytes=8 * 2**20),
        cost_estimate=pl.CostEstimate(flops=0, bytes_accessed=16 * 2**20, transcendentals=0),
    )(place, columns, ids, *pieces)


def multiply_kernel(order, found, right, left, out, left_buf, sem):
    row = pl.program_id(0)

    def fetch(r, start):
        for p in range(PER_ROW):
            copy = pltpu.make_async_copy(
                left.at[pl.ds(pl.multiple_of(order[r * PER_ROW + p], BS), BS)],
                left_buf.at[r, :, pl.ds(p * BS, BS)],
                sem.at[r],
            )
            copy.start() if start else copy.wait()

    @pl.when(row == 0)
    def first():
        for r in range(2):
            fetch(r, True)

    @pl.when(row + 2 < RG)
    def later():
        fetch(row + 2, True)

    fetch(row, False)
    lhs = left_buf[row]
    for j in range(0, JB, 2):
        rhs = jnp.concatenate(
            [
                jnp.concatenate(
                    [
                        right[pl.ds(pl.multiple_of(found[(row * PER_ROW + p) * JB + j + h], BS), BS), :]
                        for h in range(2)
                    ],
                    axis=1,
                )
                for p in range(PER_ROW)
            ],
            axis=0,
        )
        out[:, j * BS : (j + 2) * BS] = jnp.dot(lhs, rhs, preferred_element_type=jnp.float32).astype(out.dtype)


def multiply(order, found, right, left):
    smem = pl.BlockSpec(memory_space=pltpu.SMEM)
    return pl.pallas_call(
        multiply_kernel,
        grid=(RG,),
        out_shape=jax.ShapeDtypeStruct((RG * BS, JB * BS), jnp.bfloat16),
        in_specs=[smem, smem, pl.BlockSpec(memory_space=pltpu.VMEM), pl.BlockSpec(memory_space=pl.ANY)],
        out_specs=pl.BlockSpec((BS, JB * BS), lambda r: (r, 0)),
        scratch_shapes=[
            pltpu.VMEM((RG, BS, PER_ROW * BS), jnp.bfloat16),
            pltpu.SemaphoreType.DMA((RG,)),
        ],
        compiler_params=pltpu.CompilerParams(vmem_limit_bytes=16 * 2**20),
        cost_estimate=pl.CostEstimate(flops=4 * 2**30, bytes_accessed=14 * 2**20, transcendentals=0),
    )(order, found, pltpu.with_memory_space_constraint(right, pltpu.VMEM), left)


def tail(values):
    flat = values.astype(jnp.bfloat16).reshape(1, -1)
    return jnp.pad(flat, ((0, PAD - 1), (0, BS - flat.shape[1])))


def gather_right(own):
    after = lax.ppermute(own, "grp", shift_x(-1))
    before = lax.ppermute(own, "grp", shift_x(1))
    far_head = lax.ppermute(before[: R_ROWS // 2], "grp", shift_x(1))
    far_tail = lax.ppermute(after[R_ROWS // 2 :], "grp", shift_x(-1))
    mine = [own, after, far_head, far_tail, before]
    return mine + [lax.ppermute(v, "grp", SWAP_CORES) for v in mine]


def body(panel_blocks, panel_rows, panel_inner, right_blocks, right_columns):
    right = jnp.concatenate([right_blocks.reshape(R_ROWS, BS), tail(right_columns)])
    left = jnp.concatenate(
        [panel_blocks.reshape(L_ROWS, BS), tail(jnp.concatenate([panel_rows, panel_inner]))]
    )
    copies = jnp.broadcast_to(left[None], (N_Y,) + left.shape)
    line = lax.all_to_all(copies, "col", 0, 0, axis_index_groups=Y_LINES)
    lefts = lax.all_gather(line[:, :L_ROWS], "col", axis=0, tiled=True, axis_index_groups=Z_LINES)
    line_ids = tail(line[:, L_ROWS, :4])
    ids = lax.all_to_all(
        jnp.broadcast_to(line_ids[None], (N_Z,) + line_ids.shape), "col", 0, 0, axis_index_groups=Z_LINES
    )
    ids = ids[:, 0, : 4 * N_Y].astype(jnp.int32).reshape(-1)
    pieces = gather_right(right)
    columns = jnp.concatenate(
        [v[-PAD, : OWN_K * NBR] for v in pieces if v.shape[0] % BS == PAD]
    ).astype(jnp.int32)
    place = lax.axis_index("grp").reshape(1)
    rights, order, found = arrange(place, columns, ids, pieces)
    return multiply(order, found, rights, lefts.reshape(-1, BS))


def solution(mesh):
    placed = (
        P(("grp", "col"), None, None),
        P(("grp", "col")),
        P(("grp", "col")),
        P("grp", "col", None, None),
        P("grp", "col"),
    )
    return jax.shard_map(
        body, mesh=mesh, in_specs=placed, out_specs=P("grp", "col"), check_vma=False
    )
```

```python
import jax
import jax.numpy as jnp
from jax import lax
from jax.experimental import pallas as pl
from jax.experimental.pallas import tpu as pltpu
from jax.sharding import PartitionSpec as P

BS = 128
RG = 8
KS = 64
JB = 8
NBR = 4
PER_ROW = 16
N_GRP = 8
N_Y = 8
N_Z = 8
PAD = 16
OWN_K = 8
R_BLOCKS = OWN_K * NBR * BS
R_ROWS = R_BLOCKS + PAD + BS
ZERO = R_BLOCKS + PAD
L_BLOCKS = 2 * BS
L_ROWS = L_BLOCKS + PAD
MIB = 2**20
CHUNK = 4

Y_LINES = [[z * N_Y + y for y in range(N_Y)] for z in range(N_Z)]


def shift_z(step):
    return [(z * N_Y + y, ((z + step) % N_Z) * N_Y + y) for z in range(N_Z) for y in range(N_Y)]


def table_kernel(right, table, tiles, values, columns, sem):
    copies = [
        pltpu.make_async_copy(right.at[pl.ds(g * R_ROWS + R_BLOCKS, PAD)], tiles.at[g], sem.at[g])
        for g in range(N_GRP)
    ]
    for copy in copies:
        copy.start()

    def clear(i, carry):
        table[i] = ZERO
        return carry

    lax.fori_loop(0, (KS + 1) * JB, clear, 0, unroll=8)
    for copy in copies:
        copy.wait()
    values[...] = tiles[:, 0, :].astype(jnp.float32).astype(jnp.int32)
    copy = pltpu.make_async_copy(values, columns, sem.at[0])
    copy.start()
    copy.wait()

    def fill(k, carry):
        g, i = k // OWN_K, k % OWN_K
        for m in range(NBR):
            table[k * JB + columns[g, i * NBR + m]] = g * R_ROWS + (i * NBR + m) * BS
        return carry

    lax.fori_loop(0, KS, fill, 0, unroll=2)


def make_table(right):
    return pl.pallas_call(
        table_kernel,
        out_shape=jax.ShapeDtypeStruct(((KS + 1) * JB,), jnp.int32),
        in_specs=[pl.BlockSpec(memory_space=pl.ANY)],
        out_specs=pl.BlockSpec(memory_space=pltpu.SMEM),
        scratch_shapes=[
            pltpu.VMEM((N_GRP, PAD, BS), jnp.bfloat16),
            pltpu.VMEM((N_GRP, BS), jnp.int32),
            pltpu.SMEM((N_GRP, BS), jnp.int32),
            pltpu.SemaphoreType.DMA((N_GRP,)),
        ],
        compiler_params=pltpu.CompilerParams(vmem_limit_bytes=2 * MIB),
        cost_estimate=pl.CostEstimate(flops=0, bytes_accessed=MIB, transcendentals=0),
    )(pltpu.with_memory_space_constraint(right, pltpu.HBM))


def multiply_kernel(counts, later, last, table, right, *refs):
    n = len(counts)
    pieces, refs = refs[:n], refs[n:]
    if later:
        before, refs = refs[0], refs[1:]
    out, lhs, total, values, ids, inner, filled, sem = refs
    row = pl.program_id(0)
    firsts = [sum(counts[:i]) for i in range(n)]

    @pl.when(row == 0)
    def load():
        for i, piece in enumerate(pieces):
            tiles = piece[:, L_BLOCKS : L_BLOCKS + PAD, :]
            values[firsts[i] : firsts[i] + counts[i], :] = tiles[:, 0, :].astype(jnp.float32).astype(jnp.int32)
        copy = pltpu.make_async_copy(values, ids, sem.at[1])
        copy.start()
        for r in range(RG):
            filled[r] = 0
        copy.wait()
        for i, piece in enumerate(pieces):

            def place(d, carry, i=i, piece=piece):
                for b in range(2):
                    r = ids[firsts[i] + d, b]
                    p = filled[r]
                    filled[r] = p + 1
                    inner[r * PER_ROW + p] = ids[firsts[i] + d, 2 + b] * JB
                    pltpu.make_async_copy(
                        piece.at[d, pl.ds(b * BS, BS), :],
                        lhs.at[r, :, pl.ds(pl.multiple_of(p * BS, BS), BS)],
                        sem.at[0],
                    ).start()
                return carry

            lax.fori_loop(0, counts[i], place, 0, unroll=4)
        for r in range(RG):
            p = filled[r]

            def pad(q, carry, r=r):
                inner[r * PER_ROW + q] = KS * JB
                lhs[r, :, pl.ds(pl.multiple_of(q * BS, BS), BS)] = jnp.zeros((BS, BS), jnp.bfloat16)
                return carry

            lax.fori_loop(p, (p + CHUNK - 1) // CHUNK * CHUNK, pad, 0)
        whole = lhs.at[pl.ds(0, sum(counts) * 2 // PER_ROW)]
        pltpu.make_async_copy(whole, whole, sem.at[0]).wait()

    rows = pl.ds(pl.multiple_of(row * BS, BS), BS)
    if last:
        total[...] = before[rows, :]
        sums = total
    else:
        sums = out.at[rows, :]
        if not later:
            sums[...] = jnp.zeros(sums.shape, jnp.float32)

    def step(c, carry):
        a = lhs[row, :, pl.ds(pl.multiple_of(c * CHUNK * BS, CHUNK * BS), CHUNK * BS)]
        ks = [inner[row * PER_ROW + CHUNK * c + h] for h in range(CHUNK)]
        for j in range(0, JB, 2):
            b = jnp.concatenate(
                [
                    jnp.concatenate(
                        [right[pl.ds(pl.multiple_of(table[k + j + h], PAD), BS), :] for h in range(2)],
                        axis=1,
                    )
                    for k in ks
                ],
                axis=0,
            )
            sums[:, j * BS : (j + 2) * BS] += jnp.dot(a, b, preferred_element_type=jnp.float32)
        return carry

    lax.fori_loop(0, (filled[row] + CHUNK - 1) // CHUNK, step, 0)
    if last:
        out[...] = total[...].astype(out.dtype)


def multiply(table, right, pieces, before=None, last=False):
    later = before is not None
    counts = tuple(piece.shape[0] for piece in pieces)
    devices = sum(counts)
    vmem = pl.BlockSpec(memory_space=pltpu.VMEM)
    shape = (RG * BS, JB * BS)
    held = [right, *pieces] + [before] * later
    return pl.pallas_call(
        lambda *refs: multiply_kernel(counts, later, last, *refs),
        grid=(RG,),
        out_shape=jax.ShapeDtypeStruct(shape, jnp.bfloat16) if last else pltpu.VMEM(shape, jnp.float32),
        in_specs=[pl.BlockSpec(memory_space=pltpu.SMEM)] + [vmem] * len(held),
        out_specs=pl.BlockSpec((BS, JB * BS), lambda r: (r, 0)) if last else vmem,
        input_output_aliases={len(held): 0} if later and not last else {},
        scratch_shapes=[
            pltpu.VMEM((RG, BS, PER_ROW * BS), jnp.bfloat16),
            pltpu.VMEM((BS, JB * BS) if last else (8, BS), jnp.float32),
            pltpu.VMEM((devices, BS), jnp.int32),
            pltpu.SMEM((devices, BS), jnp.int32),
            pltpu.SMEM((RG * PER_ROW,), jnp.int32),
            pltpu.SMEM((RG,), jnp.int32),
            pltpu.SemaphoreType.DMA((2,)),
        ],
        compiler_params=pltpu.CompilerParams(vmem_limit_bytes=12 * MIB),
        cost_estimate=pl.CostEstimate(
            flops=devices * 2 * BS * BS * JB * BS * 2, bytes_accessed=4 * MIB, transcendentals=0
        ),
    )(table, *(pltpu.with_memory_space_constraint(v, pltpu.VMEM) for v in held))


def tail(values):
    flat = values.astype(jnp.bfloat16).reshape(1, -1)
    return jnp.pad(flat, ((0, PAD - 1), (0, BS - flat.shape[1])))


def body(panel_blocks, panel_rows, panel_inner, right_blocks, right_columns):
    right = jnp.concatenate(
        [right_blocks.reshape(R_BLOCKS, BS), tail(right_columns), jnp.zeros((BS, BS), jnp.bfloat16)]
    )
    left = jnp.concatenate(
        [panel_blocks.reshape(L_BLOCKS, BS), tail(jnp.concatenate([panel_rows, panel_inner]))]
    )
    right = lax.all_gather(right, "grp", axis=0, tiled=True)
    line = lax.all_to_all(
        jnp.broadcast_to(left[None], (N_Y,) + left.shape), "col", 0, 0, axis_index_groups=Y_LINES
    )
    up_1, down_1 = (lax.ppermute(line, "col", shift_z(s)) for s in (1, -1))
    up_2, down_2 = lax.ppermute(up_1, "col", shift_z(1)), lax.ppermute(down_1, "col", shift_z(-1))
    up_3, down_3 = lax.ppermute(up_2, "col", shift_z(1)), lax.ppermute(down_2, "col", shift_z(-1))
    right = lax.optimization_barrier((right, up_2, down_2))[0]
    table = make_table(right)
    total = multiply(table, right, [line, up_1, down_1])
    up_3, down_3, total = lax.optimization_barrier((up_3, down_3, total))
    ends = [
        lax.ppermute(up_3[: N_Y // 2], "col", shift_z(1)),
        lax.ppermute(down_3[N_Y // 2 :], "col", shift_z(-1)),
    ]
    total = multiply(table, right, [up_2, down_2, up_3, down_3], total)
    return multiply(table, right, ends, total, True)


def solution(mesh):
    placed = (
        P(("grp", "col"), None, None),
        P(("grp", "col")),
        P(("grp", "col")),
        P("grp", "col", None, None),
        P("grp", "col"),
    )
    return jax.shard_map(
        body, mesh=mesh, in_specs=placed, out_specs=P("grp", "col"), check_vma=False
    )
```

```python
import jax
import jax.numpy as jnp
from jax import lax
from jax.experimental import pallas as pl
from jax.experimental.pallas import tpu as pltpu
from jax.sharding import PartitionSpec as P

BS = 128
RG = 8
KS = 64
JB = 8
NBR = 4
PER_ROW = 16
N_X = 4
N_Y = 8
N_Z = 8
PAD = 16
OWN_K = 8
R_ROWS = OWN_K * NBR * BS
L_ROWS = 2 * BS
N_LEFT = 128
N_RIGHT = KS * NBR


def shift_x(step):
    return [(x * 2 + c, ((x + step) % N_X) * 2 + c) for x in range(N_X) for c in range(2)]


SWAP_CORES = [(g, g ^ 1) for g in range(2 * N_X)]
Y_LINES = [[z * N_Y + y for y in range(N_Y)] for z in range(N_Z)]
Z_LINES = [[z * N_Y + y for z in range(N_Z)] for y in range(N_Y)]


def multiply_kernel(place, columns, left, *refs):
    pieces, (out, right, lhs, tiles, values, ids, table, inner, filled, sem) = refs[:10], refs[10:]
    row = pl.program_id(0)

    @pl.when(row == 0)
    def load():
        heads = pltpu.make_async_copy(left.at[:, pl.ds(L_ROWS, PAD), :], tiles, sem.at[RG])
        heads.start()
        copies = []
        slot = 0
        for i, piece in enumerate(pieces):
            blocks = piece.shape[0] // BS
            copies.append(
                pltpu.make_async_copy(
                    piece.at[pl.ds(0, blocks * BS)],
                    right.at[pl.ds(slot * BS, blocks * BS)],
                    sem.at[RG + 1 + i],
                )
            )
            slot += blocks
        for copy in copies:
            copy.start()
        right[pl.ds(N_RIGHT * BS, BS), :] = jnp.zeros((BS, BS), jnp.bfloat16)
        for r in range(RG):
            filled[r] = 0
        heads.wait()
        values[...] = tiles[:, 0, :].astype(jnp.float32).astype(jnp.int32)
        heads = pltpu.make_async_copy(values, ids, sem.at[RG])
        heads.start()
        own_x, own_core = place[0] // 2, place[0] % 2

        def clear(i, carry):
            table[i] = N_RIGHT * BS
            return carry

        lax.fori_loop(0, KS * JB, clear, 0, unroll=16)
        heads.wait()

        def list_row(d, carry):
            for b in range(2):
                r = ids[d, b]
                p = filled[r]
                filled[r] = p + 1
                inner[r * PER_ROW + p] = ids[d, 2 + b] * JB
                pltpu.make_async_copy(
                    left.at[d, pl.ds(b * BS, BS), :],
                    lhs.at[r, :, pl.ds(pl.multiple_of(p * BS, BS), BS)],
                    sem.at[r],
                ).start()
            return carry

        lax.fori_loop(0, N_LEFT // 2, list_row, 0, unroll=2)

        def fill(k, carry):
            g = k // OWN_K
            s = ((g + own_core) % 2) * N_X + (g // 2 + N_X - own_x) % N_X
            first = (s * OWN_K + k % OWN_K) * NBR
            for m in range(NBR):
                table[k * JB + columns[first + m]] = (first + m) * BS
            return carry

        lax.fori_loop(0, KS, fill, 0, unroll=2)
        for copy in copies:
            copy.wait()

    strip = lhs.at[row]
    pltpu.make_async_copy(strip, strip, sem.at[row]).wait()
    ks = [inner[row * PER_ROW + p] for p in range(PER_ROW)]
    for j in range(0, JB, 2):
        rhs = jnp.concatenate(
            [
                jnp.concatenate(
                    [right[pl.ds(pl.multiple_of(table[k + j + h], BS), BS), :] for h in range(2)],
                    axis=1,
                )
                for k in ks
            ],
            axis=0,
        )
        out[:, j * BS : (j + 2) * BS] = jnp.dot(
            strip[...], rhs, preferred_element_type=jnp.float32
        ).astype(out.dtype)


def multiply(place, columns, left, pieces):
    smem = pl.BlockSpec(memory_space=pltpu.SMEM)
    hbm = pl.BlockSpec(memory_space=pl.ANY)
    devices = left.shape[0]
    return pl.pallas_call(
        multiply_kernel,
        grid=(RG,),
        out_shape=jax.ShapeDtypeStruct((RG * BS, JB * BS), jnp.bfloat16),
        in_specs=[smem] * 2 + [hbm] * (1 + len(pieces)),
        out_specs=pl.BlockSpec((BS, JB * BS), lambda r: (r, 0)),
        scratch_shapes=[
            pltpu.VMEM(((N_RIGHT + 1) * BS, BS), jnp.bfloat16),
            pltpu.VMEM((RG, BS, PER_ROW * BS), jnp.bfloat16),
            pltpu.VMEM((devices, PAD, BS), jnp.bfloat16),
            pltpu.VMEM((devices, BS), jnp.int32),
            pltpu.SMEM((devices, BS), jnp.int32),
            pltpu.SMEM((KS * JB,), jnp.int32),
            pltpu.SMEM((N_LEFT,), jnp.int32),
            pltpu.SMEM((RG,), jnp.int32),
            pltpu.SemaphoreType.DMA((RG + 1 + len(pieces),)),
        ],
        compiler_params=pltpu.CompilerParams(vmem_limit_bytes=24 * 2**20),
        cost_estimate=pl.CostEstimate(flops=4 * 2**30, bytes_accessed=14 * 2**20, transcendentals=0),
    )(place, columns, *(pltpu.with_memory_space_constraint(v, pltpu.HBM) for v in [left, *pieces]))


def tail(values):
    flat = values.astype(jnp.bfloat16).reshape(1, -1)
    return jnp.pad(flat, ((0, PAD - 1), (0, BS - flat.shape[1])))


def gather_right(own):
    after = lax.ppermute(own, "grp", shift_x(-1))
    before = lax.ppermute(own, "grp", shift_x(1))
    far_head = lax.ppermute(before[: R_ROWS // 2], "grp", shift_x(1))
    far_tail = lax.ppermute(after[R_ROWS // 2 :], "grp", shift_x(-1))
    mine = [own, after, far_head, far_tail, before]
    return mine + [lax.ppermute(v, "grp", SWAP_CORES) for v in mine]


def gather_left(own):
    copies = jnp.broadcast_to(own[None], (N_Y,) + own.shape)
    line = lax.all_to_all(copies, "col", 0, 0, axis_index_groups=Y_LINES)
    return lax.all_gather(line, "col", axis=0, tiled=True, axis_index_groups=Z_LINES)


def body(panel_blocks, panel_rows, panel_inner, right_blocks, right_columns):
    right = jnp.concatenate([right_blocks.reshape(R_ROWS, BS), tail(right_columns)])
    left = jnp.concatenate(
        [panel_blocks.reshape(L_ROWS, BS), tail(jnp.concatenate([panel_rows, panel_inner]))]
    )
    pieces = gather_right(right)
    lefts = gather_left(left)
    columns = jnp.concatenate(
        [v[-PAD, : OWN_K * NBR] for v in pieces if v.shape[0] % BS == PAD]
    ).astype(jnp.int32)
    place = lax.axis_index("grp").reshape(1)
    return multiply(place, columns, lefts, pieces)


def solution(mesh):
    placed = (
        P(("grp", "col"), None, None),
        P(("grp", "col")),
        P(("grp", "col")),
        P("grp", "col", None, None),
        P("grp", "col"),
    )
    return jax.shard_map(
        body, mesh=mesh, in_specs=placed, out_specs=P("grp", "col"), check_vma=False
    )
```

```python
import jax
import jax.numpy as jnp
from jax import lax
from jax.experimental import pallas as pl
from jax.experimental.pallas import tpu as pltpu
from jax.sharding import PartitionSpec as P

BS = 128
RG = 8
KS = 64
JB = 8
NBR = 4
PER_ROW = 16
N_GRP = 8
N_X = 4
N_Y = 8
N_Z = 8
PAD = 16
OWN_K = 8
R_ROWS = OWN_K * NBR * BS
L_ROWS = 2 * BS
N_LEFT = 128
N_RIGHT = KS * NBR


def shift_x(step):
    return [(x * 2 + c, ((x + step) % N_X) * 2 + c) for x in range(N_X) for c in range(2)]


SWAP_CORES = [(g, g ^ 1) for g in range(2 * N_X)]
Y_LINES = [[z * N_Y + y for y in range(N_Y)] for z in range(N_Z)]


def shift_z(step):
    return [(z * N_Y + y, ((z + step) % N_Z) * N_Y + y) for z in range(N_Z) for y in range(N_Y)]


def assemble_kernel(counts, *refs):
    n = len(counts)
    pieces, (strips, inner, tiles, values, ids, filled, sem) = refs[:n], refs[n:]
    firsts = [sum(counts[:i]) for i in range(n)]
    copies = [
        pltpu.make_async_copy(
            piece.at[:, pl.ds(L_ROWS, PAD), :], tiles.at[pl.ds(firsts[i], counts[i])], sem.at[i + 1]
        )
        for i, piece in enumerate(pieces)
    ]
    for copy in copies:
        copy.start()
    for r in range(RG):
        filled[r] = 0
    for copy in copies:
        copy.wait()
    values[...] = tiles[:, 0, :].astype(jnp.float32).astype(jnp.int32)
    copy = pltpu.make_async_copy(values, ids, sem.at[1])
    copy.start()
    copy.wait()
    for i, piece in enumerate(pieces):

        def place(d, carry, i=i, piece=piece):
            for b in range(2):
                r = ids[firsts[i] + d, b]
                p = filled[r]
                filled[r] = p + 1
                inner[r * PER_ROW + p] = ids[firsts[i] + d, 2 + b] * JB
                pltpu.make_async_copy(
                    piece.at[d, pl.ds(b * BS, BS), :],
                    strips.at[r, :, pl.ds(pl.multiple_of(p * BS, BS), BS)],
                    sem.at[0],
                ).start()
            return carry

        lax.fori_loop(0, counts[i], place, 0, unroll=2)
    pltpu.make_async_copy(strips, strips, sem.at[0]).wait()


def assemble(pieces):
    counts = tuple(piece.shape[0] for piece in pieces)
    devices = sum(counts)
    return pl.pallas_call(
        lambda *refs: assemble_kernel(counts, *refs),
        out_shape=(
            pltpu.VMEM((RG, BS, PER_ROW * BS), jnp.bfloat16),
            jax.ShapeDtypeStruct((N_LEFT,), jnp.int32),
        ),
        in_specs=[pl.BlockSpec(memory_space=pl.ANY)] * len(pieces),
        out_specs=(pl.BlockSpec(memory_space=pltpu.VMEM), pl.BlockSpec(memory_space=pltpu.SMEM)),
        scratch_shapes=[
            pltpu.VMEM((devices, PAD, BS), jnp.bfloat16),
            pltpu.VMEM((devices, BS), jnp.int32),
            pltpu.SMEM((devices, BS), jnp.int32),
            pltpu.SMEM((RG,), jnp.int32),
            pltpu.SemaphoreType.DMA((1 + len(pieces),)),
        ],
        compiler_params=pltpu.CompilerParams(vmem_limit_bytes=4 * 2**20),
        cost_estimate=pl.CostEstimate(flops=0, bytes_accessed=8 * 2**20, transcendentals=0),
    )(*pieces)


def multiply_kernel(place, inner, strips, *refs):
    pieces, (out, right, tiles, values, columns, table, sem) = refs[:10], refs[10:]
    row = pl.program_id(0)

    @pl.when(row == 0)
    def load():
        heads, copies = [], []
        slot = 0
        for i, piece in enumerate(pieces):
            rows = piece.shape[0]
            blocks = rows // BS
            if rows % BS:
                n = len(heads)
                heads.append(
                    pltpu.make_async_copy(piece.at[pl.ds(rows - PAD, PAD)], tiles.at[n], sem.at[10 + n])
                )
            copies.append(
                pltpu.make_async_copy(
                    piece.at[pl.ds(0, blocks * BS)], right.at[pl.ds(slot * BS, blocks * BS)], sem.at[i]
                )
            )
            slot += blocks
        for copy in heads + copies:
            copy.start()
        right[pl.ds(N_RIGHT * BS, BS), :] = jnp.zeros((BS, BS), jnp.bfloat16)
        for copy in heads:
            copy.wait()
        values[...] = tiles[:, 0, :].astype(jnp.float32).astype(jnp.int32)
        copy = pltpu.make_async_copy(values, columns, sem.at[10])
        copy.start()
        own_x, own_core = place[0] // 2, place[0] % 2

        def clear(i, carry):
            table[i] = N_RIGHT * BS
            return carry

        lax.fori_loop(0, KS * JB, clear, 0, unroll=16)
        copy.wait()

        def fill(k, carry):
            g, i = k // OWN_K, k % OWN_K
            s = ((g + own_core) % 2) * N_X + (g // 2 + N_X - own_x) % N_X
            for m in range(NBR):
                table[k * JB + columns[s, i * NBR + m]] = ((s * OWN_K + i) * NBR + m) * BS
            return carry

        lax.fori_loop(0, KS, fill, 0, unroll=2)
        for copy in copies:
            copy.wait()

    ks = [inner[row * PER_ROW + p] for p in range(PER_ROW)]
    for j in range(0, JB, 2):
        rhs = jnp.concatenate(
            [
                jnp.concatenate(
                    [right[pl.ds(pl.multiple_of(table[k + j + h], BS), BS), :] for h in range(2)],
                    axis=1,
                )
                for k in ks
            ],
            axis=0,
        )
        out[:, j * BS : (j + 2) * BS] = jnp.dot(
            strips[row], rhs, preferred_element_type=jnp.float32
        ).astype(out.dtype)


def multiply(place, inner, strips, pieces):
    smem = pl.BlockSpec(memory_space=pltpu.SMEM)
    return pl.pallas_call(
        multiply_kernel,
        grid=(RG,),
        out_shape=jax.ShapeDtypeStruct((RG * BS, JB * BS), jnp.bfloat16),
        in_specs=[smem] * 2
        + [pl.BlockSpec(memory_space=pltpu.VMEM)]
        + [pl.BlockSpec(memory_space=pl.ANY)] * len(pieces),
        out_specs=pl.BlockSpec((BS, JB * BS), lambda r: (r, 0)),
        scratch_shapes=[
            pltpu.VMEM(((N_RIGHT + 1) * BS, BS), jnp.bfloat16),
            pltpu.VMEM((N_GRP, PAD, BS), jnp.bfloat16),
            pltpu.VMEM((N_GRP, BS), jnp.int32),
            pltpu.SMEM((N_GRP, BS), jnp.int32),
            pltpu.SMEM((KS * JB,), jnp.int32),
            pltpu.SemaphoreType.DMA((10 + N_GRP,)),
        ],
        compiler_params=pltpu.CompilerParams(vmem_limit_bytes=16 * 2**20),
        cost_estimate=pl.CostEstimate(flops=4 * 2**30, bytes_accessed=14 * 2**20, transcendentals=0),
    )(place, inner, pltpu.with_memory_space_constraint(strips, pltpu.VMEM), *pieces)


def tail(values):
    flat = values.astype(jnp.bfloat16).reshape(1, -1)
    return jnp.pad(flat, ((0, PAD - 1), (0, BS - flat.shape[1])))


def gather(left, right):
    copies = jnp.broadcast_to(left[None], (N_Y,) + left.shape)
    line = lax.all_to_all(copies, "col", 0, 0, axis_index_groups=Y_LINES)
    up_1, down_1 = (lax.ppermute(line, "col", shift_z(s)) for s in (1, -1))
    after = lax.ppermute(right, "grp", shift_x(-1))
    before = lax.ppermute(right, "grp", shift_x(1))
    far_head = lax.ppermute(before[: R_ROWS // 2], "grp", shift_x(1))
    far_tail = lax.ppermute(after[R_ROWS // 2 :], "grp", shift_x(-1))
    mine = [right, after, far_head, far_tail, before]
    others = [lax.ppermute(v, "grp", SWAP_CORES) for v in mine]
    up_1, down_1 = lax.optimization_barrier((up_1, down_1, after, before))[:2]
    up_2, down_2 = lax.ppermute(up_1, "col", shift_z(1)), lax.ppermute(down_1, "col", shift_z(-1))
    up_3, down_3 = lax.ppermute(up_2, "col", shift_z(1)), lax.ppermute(down_2, "col", shift_z(-1))
    up_3, down_3 = lax.optimization_barrier((up_3, down_3, others[0], others[1], others[4]))[:2]
    ends = [
        lax.ppermute(up_3[: N_Y // 2], "col", shift_z(1)),
        lax.ppermute(down_3[N_Y // 2 :], "col", shift_z(-1)),
    ]
    return [line, up_1, down_1, up_2, down_2, up_3, down_3] + ends, mine + others


def body(panel_blocks, panel_rows, panel_inner, right_blocks, right_columns):
    right = jnp.concatenate([right_blocks.reshape(R_ROWS, BS), tail(right_columns)])
    left = jnp.concatenate(
        [panel_blocks.reshape(L_ROWS, BS), tail(jnp.concatenate([panel_rows, panel_inner]))]
    )
    lefts, pieces = gather(left, right)
    strips, inner = assemble(lefts)
    place = lax.axis_index("grp").reshape(1)
    return multiply(place, inner, strips, pieces)


def solution(mesh):
    placed = (
        P(("grp", "col"), None, None),
        P(("grp", "col")),
        P(("grp", "col")),
        P("grp", "col", None, None),
        P("grp", "col"),
    )
    return jax.shard_map(
        body, mesh=mesh, in_specs=placed, out_specs=P("grp", "col"), check_vma=False
    )
```

```python
import jax
import jax.numpy as jnp
from jax import lax
from jax.experimental import pallas as pl
from jax.experimental.pallas import tpu as pltpu
from jax.sharding import PartitionSpec as P

BS = 128
RG = 8
KS = 64
JB = 8
NBR = 4
PER_ROW = 16
N_GRP = 8
N_X = 4
N_Y = 8
N_Z = 8
PAD = 16
OWN_K = 8
R_ROWS = OWN_K * NBR * BS
L_ROWS = 2 * BS
REST = 32
N_LEFT = 128
N_RIGHT = KS * NBR


def shift_x(step):
    return [(x * 2 + c, ((x + step) % N_X) * 2 + c) for x in range(N_X) for c in range(2)]


SWAP_CORES = [(g, g ^ 1) for g in range(2 * N_X)]
Y_LINES = [[z * N_Y + y for y in range(N_Y)] for z in range(N_Z)]
Z_LINES = [[z * N_Y + y for z in range(N_Z)] for y in range(N_Y)]


def arrange_kernel(place, *refs):
    pieces, (right, table, zeros, tiles, values, columns, sem) = refs[:10], refs[10:]
    zeros[...] = jnp.zeros((BS, BS), jnp.bfloat16)
    heads, copies = [], [pltpu.make_async_copy(zeros, right.at[pl.ds(N_RIGHT * BS, BS)], sem.at[10])]
    slot = 0
    for i, piece in enumerate(pieces):
        rows = piece.shape[0]
        blocks = rows // BS
        if rows % BS:
            n = len(heads)
            heads.append(pltpu.make_async_copy(piece.at[pl.ds(rows - PAD, PAD)], tiles.at[n], sem.at[11 + n]))
        copies.append(
            pltpu.make_async_copy(
                piece.at[pl.ds(0, blocks * BS)], right.at[pl.ds(slot * BS, blocks * BS)], sem.at[i]
            )
        )
        slot += blocks
    for copy in heads + copies:
        copy.start()
    for copy in heads:
        copy.wait()
    values[...] = tiles[:, 0, :].astype(jnp.float32).astype(jnp.int32)
    copy = pltpu.make_async_copy(values, columns, sem.at[11])
    copy.start()
    own_x, own_core = place[0] // 2, place[0] % 2

    def clear(i, carry):
        table[i] = N_RIGHT * BS
        return carry

    lax.fori_loop(0, KS * JB, clear, 0, unroll=16)
    copy.wait()

    def fill(k, carry):
        g, i = k // OWN_K, k % OWN_K
        s = ((g + own_core) % 2) * N_X + (g // 2 + N_X - own_x) % N_X
        for m in range(NBR):
            table[k * JB + columns[s, i * NBR + m]] = ((s * OWN_K + i) * NBR + m) * BS
        return carry

    lax.fori_loop(0, KS, fill, 0, unroll=2)
    for copy in copies:
        copy.wait()


def arrange(place, pieces):
    smem = pl.BlockSpec(memory_space=pltpu.SMEM)
    hbm = pl.BlockSpec(memory_space=pl.ANY)
    return pl.pallas_call(
        arrange_kernel,
        out_shape=(
            pltpu.HBM(((N_RIGHT + 1) * BS, BS), jnp.bfloat16),
            jax.ShapeDtypeStruct((KS * JB,), jnp.int32),
        ),
        in_specs=[smem] + [hbm] * len(pieces),
        out_specs=(hbm, smem),
        scratch_shapes=[
            pltpu.VMEM((BS, BS), jnp.bfloat16),
            pltpu.VMEM((N_GRP, PAD, BS), jnp.bfloat16),
            pltpu.VMEM((N_GRP, BS), jnp.int32),
            pltpu.SMEM((N_GRP, BS), jnp.int32),
            pltpu.SemaphoreType.DMA((11 + N_GRP,)),
        ],
        compiler_params=pltpu.CompilerParams(vmem_limit_bytes=4 * 2**20),
        cost_estimate=pl.CostEstimate(flops=2**0, bytes_accessed=16 * 2**20, transcendentals=0),
    )(place, *pieces)


def multiply_kernel(table, right, left, rest, out, held, strips, tiles, values, ids, inner, filled, sem):
    row = pl.program_id(0)

    @pl.when(row == 0)
    def load():
        heads = pltpu.make_async_copy(rest.at[:, :, pl.ds(REST, PAD), :], tiles, sem.at[RG])
        heads.start()
        part = N_RIGHT * BS // 8
        copies = [
            pltpu.make_async_copy(
                right.at[pl.ds(i * part, part)], held.at[pl.ds(i * part, part)], sem.at[RG + 1 + i]
            )
            for i in range(8)
        ]
        for copy in copies:
            copy.start()
        held[pl.ds(N_RIGHT * BS, BS), :] = jnp.zeros((BS, BS), jnp.bfloat16)
        for r in range(RG):
            filled[r] = 0
        heads.wait()
        for y in range(N_Y):
            values[y * N_Z : (y + 1) * N_Z, :] = tiles[y, :, 0, :].astype(jnp.float32).astype(jnp.int32)
        heads = pltpu.make_async_copy(values, ids, sem.at[RG])
        heads.start()
        heads.wait()

        def list_row(n, carry):
            y, z = n // N_Z, n % N_Z
            d = z * N_Y + y
            for b in range(2):
                r = ids[n, b]
                p = filled[r]
                filled[r] = p + 1
                inner[r * PER_ROW + p] = ids[n, 2 + b] * JB
                column = pl.ds(pl.multiple_of(p * BS, BS), BS)
                rows = BS - REST * b
                pltpu.make_async_copy(
                    left.at[d, pl.ds(b * BS, rows), :], strips.at[r, pl.ds(0, rows), column], sem.at[r]
                ).start()
                if b:
                    pltpu.make_async_copy(
                        rest.at[y, z, pl.ds(0, REST), :], strips.at[r, pl.ds(rows, REST), column], sem.at[r]
                    ).start()
            return carry

        lax.fori_loop(0, N_LEFT // 2, list_row, 0, unroll=2)
        for copy in copies:
            copy.wait()

    strip = strips.at[row]
    pltpu.make_async_copy(strip, strip, sem.at[row]).wait()
    ks = [inner[row * PER_ROW + p] for p in range(PER_ROW)]
    for j in range(0, JB, 2):
        rhs = jnp.concatenate(
            [
                jnp.concatenate(
                    [held[pl.ds(pl.multiple_of(table[k + j + h], BS), BS), :] for h in range(2)],
                    axis=1,
                )
                for k in ks
            ],
            axis=0,
        )
        out[:, j * BS : (j + 2) * BS] = jnp.dot(
            strip[...], rhs, preferred_element_type=jnp.float32
        ).astype(out.dtype)


def multiply(table, right, left, rest):
    hbm = pl.BlockSpec(memory_space=pl.ANY)
    devices = left.shape[0]
    return pl.pallas_call(
        multiply_kernel,
        grid=(RG,),
        out_shape=jax.ShapeDtypeStruct((RG * BS, JB * BS), jnp.bfloat16),
        in_specs=[pl.BlockSpec(memory_space=pltpu.SMEM)] + [hbm] * 3,
        out_specs=pl.BlockSpec((BS, JB * BS), lambda r: (r, 0)),
        scratch_shapes=[
            pltpu.VMEM(((N_RIGHT + 1) * BS, BS), jnp.bfloat16),
            pltpu.VMEM((RG, BS, PER_ROW * BS), jnp.bfloat16),
            pltpu.VMEM((N_Y, N_Z, PAD, BS), jnp.bfloat16),
            pltpu.VMEM((devices, BS), jnp.int32),
            pltpu.SMEM((devices, BS), jnp.int32),
            pltpu.SMEM((N_LEFT,), jnp.int32),
            pltpu.SMEM((RG,), jnp.int32),
            pltpu.SemaphoreType.DMA((RG + 9,)),
        ],
        compiler_params=pltpu.CompilerParams(vmem_limit_bytes=24 * 2**20),
        cost_estimate=pl.CostEstimate(flops=4 * 2**30, bytes_accessed=14 * 2**20, transcendentals=0),
    )(table, *(pltpu.with_memory_space_constraint(v, pltpu.HBM) for v in [right, left, rest]))


def tail(values):
    flat = values.astype(jnp.bfloat16).reshape(1, -1)
    return jnp.pad(flat, ((0, PAD - 1), (0, BS - flat.shape[1])))


def gather_right(own):
    after = lax.ppermute(own, "grp", shift_x(-1))
    before = lax.ppermute(own, "grp", shift_x(1))
    far_head = lax.ppermute(before[: R_ROWS // 2], "grp", shift_x(1))
    far_tail = lax.ppermute(after[R_ROWS // 2 :], "grp", shift_x(-1))
    mine = [own, after, far_head, far_tail, before]
    return mine + [lax.ppermute(v, "grp", SWAP_CORES) for v in mine]


def spread(own, lines):
    copies = jnp.broadcast_to(own[None], (len(lines[0]),) + own.shape)
    return lax.all_to_all(copies, "col", 0, 0, axis_index_groups=lines)


def body(panel_blocks, panel_rows, panel_inner, right_blocks, right_columns):
    right = jnp.concatenate([right_blocks.reshape(R_ROWS, BS), tail(right_columns)])
    left = panel_blocks.reshape(L_ROWS, BS)
    line = spread(left[: L_ROWS - REST], Y_LINES)
    lefts = lax.all_gather(line, "col", axis=0, tiled=True, axis_index_groups=Z_LINES)
    rest = jnp.concatenate([left[L_ROWS - REST :], tail(jnp.concatenate([panel_rows, panel_inner]))])
    rest = lax.optimization_barrier((rest, line))[0]
    rest = spread(spread(rest, Z_LINES), Y_LINES)
    place = lax.axis_index("grp").reshape(1)
    rights, table = arrange(place, gather_right(right))
    return multiply(table, rights, lefts, rest)


def solution(mesh):
    placed = (
        P(("grp", "col"), None, None),
        P(("grp", "col")),
        P(("grp", "col")),
        P("grp", "col", None, None),
        P("grp", "col"),
    )
    return jax.shard_map(
        body, mesh=mesh, in_specs=placed, out_specs=P("grp", "col"), check_vma=False
    )
```

```python
import jax
import jax.numpy as jnp
from jax import lax
from jax.experimental import pallas as pl
from jax.experimental.pallas import tpu as pltpu
from jax.sharding import PartitionSpec as P

BS = 128
RG = 8
KS = 64
JB = 8
NBR = 4
PER_ROW = 16
N_GRP = 8
N_X = 4
N_Y = 8
N_Z = 8
PAD = 16
OWN_K = 8
R_ROWS = OWN_K * NBR * BS
L_ROWS = 2 * BS
REST = 32
N_LEFT = 128
N_RIGHT = KS * NBR


def shift_x(step):
    return [(x * 2 + c, ((x + step) % N_X) * 2 + c) for x in range(N_X) for c in range(2)]


SWAP_CORES = [(g, g ^ 1) for g in range(2 * N_X)]
Y_LINES = [[z * N_Y + y for y in range(N_Y)] for z in range(N_Z)]
Z_LINES = [[z * N_Y + y for z in range(N_Z)] for y in range(N_Y)]


def table_kernel(place, *refs):
    pieces, (table, tiles, values, columns, sem) = refs[:10], refs[10:]
    pieces = [piece for piece in pieces if piece.shape[0] % BS]
    heads = [
        pltpu.make_async_copy(piece.at[pl.ds(piece.shape[0] - PAD, PAD)], tiles.at[n], sem.at[n])
        for n, piece in enumerate(pieces)
    ]
    for copy in heads:
        copy.start()
    for copy in heads:
        copy.wait()
    values[...] = tiles[:, 0, :].astype(jnp.float32).astype(jnp.int32)
    copy = pltpu.make_async_copy(values, columns, sem.at[0])
    copy.start()
    own_x, own_core = place[0] // 2, place[0] % 2

    def clear(i, carry):
        table[i] = N_RIGHT * BS
        return carry

    lax.fori_loop(0, KS * JB, clear, 0, unroll=16)
    copy.wait()

    def fill(k, carry):
        g, i = k // OWN_K, k % OWN_K
        s = ((g + own_core) % 2) * N_X + (g // 2 + N_X - own_x) % N_X
        for m in range(NBR):
            table[k * JB + columns[s, i * NBR + m]] = ((s * OWN_K + i) * NBR + m) * BS
        return carry

    lax.fori_loop(0, KS, fill, 0, unroll=2)


def make_table(place, pieces):
    smem = pl.BlockSpec(memory_space=pltpu.SMEM)
    hbm = pl.BlockSpec(memory_space=pl.ANY)
    return pl.pallas_call(
        table_kernel,
        out_shape=jax.ShapeDtypeStruct((KS * JB,), jnp.int32),
        in_specs=[smem] + [hbm] * len(pieces),
        out_specs=smem,
        scratch_shapes=[
            pltpu.VMEM((N_GRP, PAD, BS), jnp.bfloat16),
            pltpu.VMEM((N_GRP, BS), jnp.int32),
            pltpu.SMEM((N_GRP, BS), jnp.int32),
            pltpu.SemaphoreType.DMA((N_GRP,)),
        ],
        compiler_params=pltpu.CompilerParams(vmem_limit_bytes=2 * 2**20),
        cost_estimate=pl.CostEstimate(flops=48 * 2**30, bytes_accessed=2**20, transcendentals=0),
    )(place, *pieces)


def list_kernel(rest, spots, inner, tiles, values, ids, filled, sem):
    copy = pltpu.make_async_copy(rest.at[:, :, pl.ds(REST, PAD), :], tiles, sem.at[0])
    copy.start()
    for r in range(RG):
        filled[r] = 0
    copy.wait()
    for y in range(N_Y):
        values[y * N_Z : (y + 1) * N_Z, :] = tiles[y, :, 0, :].astype(jnp.float32).astype(jnp.int32)
    copy = pltpu.make_async_copy(values, ids, sem.at[0])
    copy.start()
    copy.wait()

    def list_row(n, carry):
        for b in range(2):
            r = ids[n, b]
            p = filled[r]
            filled[r] = p + 1
            spots[2 * n + b] = r * PER_ROW + p
            inner[r * PER_ROW + p] = ids[n, 2 + b] * JB
        return carry

    lax.fori_loop(0, N_LEFT // 2, list_row, 0, unroll=2)


def make_lists(rest):
    smem = pl.BlockSpec(memory_space=pltpu.SMEM)
    devices = N_Y * N_Z
    return pl.pallas_call(
        list_kernel,
        out_shape=[jax.ShapeDtypeStruct((N_LEFT,), jnp.int32)] * 2,
        in_specs=[pl.BlockSpec(memory_space=pl.ANY)],
        out_specs=[smem] * 2,
        scratch_shapes=[
            pltpu.VMEM((N_Y, N_Z, PAD, BS), jnp.bfloat16),
            pltpu.VMEM((devices, BS), jnp.int32),
            pltpu.SMEM((devices, BS), jnp.int32),
            pltpu.SMEM((RG,), jnp.int32),
            pltpu.SemaphoreType.DMA((1,)),
        ],
        compiler_params=pltpu.CompilerParams(vmem_limit_bytes=2 * 2**20),
        cost_estimate=pl.CostEstimate(flops=0 * 2**30, bytes_accessed=2**20, transcendentals=0),
    )(rest)


def multiply_kernel(table, spots, inner, left, rest, *refs):
    pieces, (out, held, strips, sem) = refs[:10], refs[10:]
    row = pl.program_id(0)

    @pl.when(row == 0)
    def load():
        copies = []
        slot = 0
        for i, piece in enumerate(pieces):
            blocks = piece.shape[0] // BS
            copies.append(
                pltpu.make_async_copy(
                    piece.at[pl.ds(0, blocks * BS)],
                    held.at[pl.ds(slot * BS, blocks * BS)],
                    sem.at[RG + i],
                )
            )
            slot += blocks
        for copy in copies:
            copy.start()
        held[pl.ds(N_RIGHT * BS, BS), :] = jnp.zeros((BS, BS), jnp.bfloat16)

        def list_row(n, carry):
            y, z = n // N_Z, n % N_Z
            d = z * N_Y + y
            for b in range(2):
                r, p = spots[2 * n + b] // PER_ROW, spots[2 * n + b] % PER_ROW
                column = pl.ds(pl.multiple_of(p * BS, BS), BS)
                rows = BS - REST * b
                pltpu.make_async_copy(
                    left.at[d, pl.ds(b * BS, rows), :], strips.at[r, pl.ds(0, rows), column], sem.at[r]
                ).start()
                if b:
                    pltpu.make_async_copy(
                        rest.at[y, z, pl.ds(0, REST), :], strips.at[r, pl.ds(rows, REST), column], sem.at[r]
                    ).start()
            return carry

        lax.fori_loop(0, N_LEFT // 2, list_row, 0, unroll=2)
        for copy in copies:
            copy.wait()

    strip = strips.at[row]
    pltpu.make_async_copy(strip, strip, sem.at[row]).wait()
    ks = [inner[row * PER_ROW + p] for p in range(PER_ROW)]
    for j in range(0, JB, 2):
        rhs = jnp.concatenate(
            [
                jnp.concatenate(
                    [held[pl.ds(pl.multiple_of(table[k + j + h], BS), BS), :] for h in range(2)],
                    axis=1,
                )
                for k in ks
            ],
            axis=0,
        )
        out[:, j * BS : (j + 2) * BS] = jnp.dot(
            strip[...], rhs, preferred_element_type=jnp.float32
        ).astype(out.dtype)


def multiply(table, lists, left, rest, pieces):
    hbm = pl.BlockSpec(memory_space=pl.ANY)
    return pl.pallas_call(
        multiply_kernel,
        grid=(RG,),
        out_shape=jax.ShapeDtypeStruct((RG * BS, JB * BS), jnp.bfloat16),
        in_specs=[pl.BlockSpec(memory_space=pltpu.SMEM)] * 3 + [hbm] * (2 + len(pieces)),
        out_specs=pl.BlockSpec((BS, JB * BS), lambda r: (r, 0)),
        scratch_shapes=[
            pltpu.VMEM(((N_RIGHT + 1) * BS, BS), jnp.bfloat16),
            pltpu.VMEM((RG, BS, PER_ROW * BS), jnp.bfloat16),
            pltpu.SemaphoreType.DMA((RG + len(pieces),)),
        ],
        compiler_params=pltpu.CompilerParams(vmem_limit_bytes=24 * 2**20),
        cost_estimate=pl.CostEstimate(flops=4 * 2**30, bytes_accessed=14 * 2**20, transcendentals=0),
    )(table, *lists, *(pltpu.with_memory_space_constraint(v, pltpu.HBM) for v in [left, rest, *pieces]))


def tail(values):
    flat = values.astype(jnp.bfloat16).reshape(1, -1)
    return jnp.pad(flat, ((0, PAD - 1), (0, BS - flat.shape[1])))


def gather_right(own, first, second):
    after = lax.ppermute(own, "grp", shift_x(-1))
    before = lax.ppermute(own, "grp", shift_x(1))
    onward, back = lax.optimization_barrier((before, after, first))[:2]
    far_head = lax.ppermute(onward[: R_ROWS // 2], "grp", shift_x(1))
    far_tail = lax.ppermute(back[R_ROWS // 2 :], "grp", shift_x(-1))
    mine = [own, after, far_head, far_tail, before]
    far_head, far_tail = lax.optimization_barrier((far_head, far_tail, second))[:2]
    others = [own, after, far_head, far_tail, before]
    return mine + [lax.ppermute(v, "grp", SWAP_CORES) for v in others]


def spread(own, lines):
    copies = jnp.broadcast_to(own[None], (len(lines[0]),) + own.shape)
    return lax.all_to_all(copies, "col", 0, 0, axis_index_groups=lines)


def body(panel_blocks, panel_rows, panel_inner, right_blocks, right_columns):
    right = jnp.concatenate([right_blocks.reshape(R_ROWS, BS), tail(right_columns)])
    left = panel_blocks.reshape(L_ROWS, BS)
    line = spread(left[: L_ROWS - REST], Y_LINES)
    lefts = lax.all_gather(line, "col", axis=0, tiled=True, axis_index_groups=Z_LINES)
    rest = jnp.concatenate([left[L_ROWS - REST :], tail(jnp.concatenate([panel_rows, panel_inner]))])
    rest = lax.optimization_barrier((rest, line))[0]
    strip = spread(rest, Z_LINES)
    rest = spread(strip, Y_LINES)
    pieces = gather_right(right, strip, rest)
    place = lax.axis_index("grp").reshape(1)
    table = make_table(place, pieces)
    return multiply(table, make_lists(rest), lefts, rest, pieces)


def solution(mesh):
    placed = (
        P(("grp", "col"), None, None),
        P(("grp", "col")),
        P(("grp", "col")),
        P("grp", "col", None, None),
        P("grp", "col"),
    )
    return jax.shard_map(
        body, mesh=mesh, in_specs=placed, out_specs=P("grp", "col"), check_vma=False
    )
```

```python
import jax
import jax.numpy as jnp
from jax import lax
from jax.experimental import pallas as pl
from jax.experimental.pallas import tpu as pltpu
from jax.sharding import PartitionSpec as P

BS = 128
RG = 8
KS = 64
JB = 8
NBR = 4
PER_ROW = 16
N_GRP = 8
N_X = 4
N_Y = 8
N_Z = 8
PAD = 16
OWN_K = 8
R_ROWS = OWN_K * NBR * BS
L_ROWS = 2 * BS
REST = 32
N_LEFT = 128
N_RIGHT = KS * NBR


def shift_x(step):
    return [(x * 2 + c, ((x + step) % N_X) * 2 + c) for x in range(N_X) for c in range(2)]


SWAP_CORES = [(g, g ^ 1) for g in range(2 * N_X)]
Y_LINES = [[z * N_Y + y for y in range(N_Y)] for z in range(N_Z)]
Z_LINES = [[z * N_Y + y for z in range(N_Z)] for y in range(N_Y)]


def table_kernel(place, *refs):
    pieces, (table, tiles, values, columns, sem) = refs[:10], refs[10:]
    pieces = [piece for piece in pieces if piece.shape[0] % BS]
    heads = [
        pltpu.make_async_copy(piece.at[pl.ds(piece.shape[0] - PAD, PAD)], tiles.at[n], sem.at[n])
        for n, piece in enumerate(pieces)
    ]
    for copy in heads:
        copy.start()
    for copy in heads:
        copy.wait()
    values[...] = tiles[:, 0, :].astype(jnp.float32).astype(jnp.int32)
    copy = pltpu.make_async_copy(values, columns, sem.at[0])
    copy.start()
    own_x, own_core = place[0] // 2, place[0] % 2

    def clear(i, carry):
        table[i] = N_RIGHT * BS
        return carry

    lax.fori_loop(0, KS * JB, clear, 0, unroll=16)
    copy.wait()

    def fill(k, carry):
        g, i = k // OWN_K, k % OWN_K
        s = ((g + own_core) % 2) * N_X + (g // 2 + N_X - own_x) % N_X
        for m in range(NBR):
            table[k * JB + columns[s, i * NBR + m]] = ((s * OWN_K + i) * NBR + m) * BS
        return carry

    lax.fori_loop(0, KS, fill, 0, unroll=2)


def make_table(place, pieces):
    smem = pl.BlockSpec(memory_space=pltpu.SMEM)
    hbm = pl.BlockSpec(memory_space=pl.ANY)
    return pl.pallas_call(
        table_kernel,
        out_shape=jax.ShapeDtypeStruct((KS * JB,), jnp.int32),
        in_specs=[smem] + [hbm] * len(pieces),
        out_specs=smem,
        scratch_shapes=[
            pltpu.VMEM((N_GRP, PAD, BS), jnp.bfloat16),
            pltpu.VMEM((N_GRP, BS), jnp.int32),
            pltpu.SMEM((N_GRP, BS), jnp.int32),
            pltpu.SemaphoreType.DMA((N_GRP,)),
        ],
        compiler_params=pltpu.CompilerParams(vmem_limit_bytes=2 * 2**20),
        cost_estimate=pl.CostEstimate(flops=40 * 2**30, bytes_accessed=2**20, transcendentals=0),
    )(place, *pieces)


def list_kernel(rest, spots, inner, tiles, values, ids, filled, sem):
    copy = pltpu.make_async_copy(rest.at[:, :, pl.ds(REST, PAD), :], tiles, sem.at[0])
    copy.start()
    for r in range(RG):
        filled[r] = 0
    copy.wait()
    for y in range(N_Y):
        values[y * N_Z : (y + 1) * N_Z, :] = tiles[y, :, 0, :].astype(jnp.float32).astype(jnp.int32)
    copy = pltpu.make_async_copy(values, ids, sem.at[0])
    copy.start()
    copy.wait()

    def list_row(n, carry):
        for b in range(2):
            r = ids[n, b]
            p = filled[r]
            filled[r] = p + 1
            spots[2 * n + b] = r * PER_ROW + p
            inner[r * PER_ROW + p] = ids[n, 2 + b] * JB
        return carry

    lax.fori_loop(0, N_LEFT // 2, list_row, 0, unroll=2)


def make_lists(rest):
    smem = pl.BlockSpec(memory_space=pltpu.SMEM)
    devices = N_Y * N_Z
    return pl.pallas_call(
        list_kernel,
        out_shape=[jax.ShapeDtypeStruct((N_LEFT,), jnp.int32)] * 2,
        in_specs=[pl.BlockSpec(memory_space=pl.ANY)],
        out_specs=[smem] * 2,
        scratch_shapes=[
            pltpu.VMEM((N_Y, N_Z, PAD, BS), jnp.bfloat16),
            pltpu.VMEM((devices, BS), jnp.int32),
            pltpu.SMEM((devices, BS), jnp.int32),
            pltpu.SMEM((RG,), jnp.int32),
            pltpu.SemaphoreType.DMA((1,)),
        ],
        compiler_params=pltpu.CompilerParams(vmem_limit_bytes=2 * 2**20),
        cost_estimate=pl.CostEstimate(flops=0, bytes_accessed=2**20, transcendentals=0),
    )(rest)


def multiply_kernel(table, spots, inner, left, rest, *refs):
    pieces, (out, held, strips, sem) = refs[:10], refs[10:]
    row = pl.program_id(0)

    @pl.when(row == 0)
    def load():
        copies = []
        slot = 0
        for i, piece in enumerate(pieces):
            blocks = piece.shape[0] // BS
            copies.append(
                pltpu.make_async_copy(
                    piece.at[pl.ds(0, blocks * BS)],
                    held.at[pl.ds(slot * BS, blocks * BS)],
                    sem.at[RG + i],
                )
            )
            slot += blocks
        for copy in copies:
            copy.start()
        held[pl.ds(N_RIGHT * BS, BS), :] = jnp.zeros((BS, BS), jnp.bfloat16)

        def list_row(n, carry):
            y, z = n // N_Z, n % N_Z
            d = z * N_Y + y
            for b in range(2):
                r, p = spots[2 * n + b] // PER_ROW, spots[2 * n + b] % PER_ROW
                column = pl.ds(pl.multiple_of(p * BS, BS), BS)
                rows = BS - REST * b
                pltpu.make_async_copy(
                    left.at[d, pl.ds(b * BS, rows), :], strips.at[r, pl.ds(0, rows), column], sem.at[r]
                ).start()
                if b:
                    pltpu.make_async_copy(
                        rest.at[y, z, pl.ds(0, REST), :], strips.at[r, pl.ds(rows, REST), column], sem.at[r]
                    ).start()
            return carry

        lax.fori_loop(0, N_LEFT // 2, list_row, 0, unroll=2)
        for copy in copies:
            copy.wait()

    strip = strips.at[row]
    pltpu.make_async_copy(strip, strip, sem.at[row]).wait()
    ks = [inner[row * PER_ROW + p] for p in range(PER_ROW)]
    for j in range(0, JB, 2):
        rhs = jnp.concatenate(
            [
                jnp.concatenate(
                    [held[pl.ds(pl.multiple_of(table[k + j + h], BS), BS), :] for h in range(2)],
                    axis=1,
                )
                for k in ks
            ],
            axis=0,
        )
        out[:, j * BS : (j + 2) * BS] = jnp.dot(
            strip[...], rhs, preferred_element_type=jnp.float32
        ).astype(out.dtype)


def multiply(table, lists, left, rest, pieces):
    hbm = pl.BlockSpec(memory_space=pl.ANY)
    return pl.pallas_call(
        multiply_kernel,
        grid=(RG,),
        out_shape=jax.ShapeDtypeStruct((RG * BS, JB * BS), jnp.bfloat16),
        in_specs=[pl.BlockSpec(memory_space=pltpu.SMEM)] * 3 + [hbm] * (2 + len(pieces)),
        out_specs=pl.BlockSpec((BS, JB * BS), lambda r: (r, 0)),
        scratch_shapes=[
            pltpu.VMEM(((N_RIGHT + 1) * BS, BS), jnp.bfloat16),
            pltpu.VMEM((RG, BS, PER_ROW * BS), jnp.bfloat16),
            pltpu.SemaphoreType.DMA((RG + len(pieces),)),
        ],
        compiler_params=pltpu.CompilerParams(vmem_limit_bytes=24 * 2**20),
        cost_estimate=pl.CostEstimate(flops=4 * 2**30, bytes_accessed=14 * 2**20, transcendentals=0),
    )(table, *lists, *(pltpu.with_memory_space_constraint(v, pltpu.HBM) for v in [left, rest, *pieces]))


def tail(values):
    flat = values.astype(jnp.bfloat16).reshape(1, -1)
    return jnp.pad(flat, ((0, PAD - 1), (0, BS - flat.shape[1])))


def gather_right(own, first, second):
    after = lax.ppermute(own, "grp", shift_x(-1))
    before = lax.ppermute(own, "grp", shift_x(1))
    onward, back = lax.optimization_barrier((before, after, first))[:2]
    far_head = lax.ppermute(onward[: R_ROWS // 2], "grp", shift_x(1))
    far_tail = lax.ppermute(back[R_ROWS // 2 :], "grp", shift_x(-1))
    mine = [own, after, far_head, far_tail, before]
    far_head, far_tail = lax.optimization_barrier((far_head, far_tail, second))[:2]
    others = [own, after, far_head, far_tail, before]
    return mine + [lax.ppermute(v, "grp", SWAP_CORES) for v in others]


def spread(own, lines):
    copies = jnp.broadcast_to(own[None], (len(lines[0]),) + own.shape)
    return lax.all_to_all(copies, "col", 0, 0, axis_index_groups=lines)


def body(panel_blocks, panel_rows, panel_inner, right_blocks, right_columns):
    right = jnp.concatenate([right_blocks.reshape(R_ROWS, BS), tail(right_columns)])
    left = panel_blocks.reshape(L_ROWS, BS)
    line = spread(left[: L_ROWS - REST], Y_LINES)
    lefts = lax.all_gather(line, "col", axis=0, tiled=True, axis_index_groups=Z_LINES)
    rest = jnp.concatenate([left[L_ROWS - REST :], tail(jnp.concatenate([panel_rows, panel_inner]))])
    rest = lax.optimization_barrier((rest, line))[0]
    strip = spread(rest, Z_LINES)
    rest = spread(strip, Y_LINES)
    pieces = gather_right(right, strip, rest)
    place = lax.axis_index("grp").reshape(1)
    table = make_table(place, pieces)
    return multiply(table, make_lists(rest), lefts, rest, pieces)


def solution(mesh):
    placed = (
        P(("grp", "col"), None, None),
        P(("grp", "col")),
        P(("grp", "col")),
        P("grp", "col", None, None),
        P("grp", "col"),
    )
    return jax.shard_map(
        body, mesh=mesh, in_specs=placed, out_specs=P("grp", "col"), check_vma=False
    )
```

```python
import jax
import jax.numpy as jnp
from jax import lax
from jax.experimental import pallas as pl
from jax.experimental.pallas import tpu as pltpu
from jax.sharding import PartitionSpec as P

BS = 128
RG = 8
KS = 64
JB = 8
NBR = 4
PER_ROW = 16
N_GRP = 8
N_X = 4
N_Y = 8
N_Z = 8
PAD = 16
OWN_K = 8
R_ROWS = OWN_K * NBR * BS
L_ROWS = 2 * BS
REST = 32
N_LEFT = 128
N_RIGHT = KS * NBR


def shift_x(step):
    return [(x * 2 + c, ((x + step) % N_X) * 2 + c) for x in range(N_X) for c in range(2)]


SWAP_CORES = [(g, g ^ 1) for g in range(2 * N_X)]
Y_LINES = [[z * N_Y + y for y in range(N_Y)] for z in range(N_Z)]
Z_LINES = [[z * N_Y + y for z in range(N_Z)] for y in range(N_Y)]


def columns_kernel(*refs):
    pieces, (columns, tiles, values, sem) = refs[:10], refs[10:]
    pieces = [piece for piece in pieces if piece.shape[0] % BS]
    heads = [
        pltpu.make_async_copy(piece.at[pl.ds(piece.shape[0] - PAD, PAD)], tiles.at[n], sem.at[n])
        for n, piece in enumerate(pieces)
    ]
    for copy in heads:
        copy.start()
    for copy in heads:
        copy.wait()
    values[...] = tiles[:, 0, :].astype(jnp.float32).astype(jnp.int32)
    copy = pltpu.make_async_copy(values, columns, sem.at[0])
    copy.start()
    copy.wait()


def read_columns(pieces):
    smem = pl.BlockSpec(memory_space=pltpu.SMEM)
    hbm = pl.BlockSpec(memory_space=pl.ANY)
    return pl.pallas_call(
        columns_kernel,
        out_shape=jax.ShapeDtypeStruct((N_GRP, BS), jnp.int32),
        in_specs=[hbm] * len(pieces),
        out_specs=smem,
        scratch_shapes=[
            pltpu.VMEM((N_GRP, PAD, BS), jnp.bfloat16),
            pltpu.VMEM((N_GRP, BS), jnp.int32),
            pltpu.SemaphoreType.DMA((N_GRP,)),
        ],
        compiler_params=pltpu.CompilerParams(vmem_limit_bytes=2 * 2**20),
        cost_estimate=pl.CostEstimate(flops=40 * 2**30, bytes_accessed=2**20, transcendentals=0),
    )(*pieces)


def list_kernel(rest, spots, inner, tiles, values, ids, filled, sem):
    copy = pltpu.make_async_copy(rest.at[:, :, pl.ds(REST, PAD), :], tiles, sem.at[0])
    copy.start()
    for r in range(RG):
        filled[r] = 0
    copy.wait()
    for y in range(N_Y):
        values[y * N_Z : (y + 1) * N_Z, :] = tiles[y, :, 0, :].astype(jnp.float32).astype(jnp.int32)
    copy = pltpu.make_async_copy(values, ids, sem.at[0])
    copy.start()
    copy.wait()

    def list_row(n, carry):
        for b in range(2):
            r = ids[n, b]
            p = filled[r]
            filled[r] = p + 1
            spots[2 * n + b] = r * PER_ROW + p
            inner[r * PER_ROW + p] = ids[n, 2 + b] * JB
        return carry

    lax.fori_loop(0, N_LEFT // 2, list_row, 0, unroll=2)


def make_lists(rest):
    smem = pl.BlockSpec(memory_space=pltpu.SMEM)
    devices = N_Y * N_Z
    return pl.pallas_call(
        list_kernel,
        out_shape=[jax.ShapeDtypeStruct((N_LEFT,), jnp.int32)] * 2,
        in_specs=[pl.BlockSpec(memory_space=pl.ANY)],
        out_specs=[smem] * 2,
        scratch_shapes=[
            pltpu.VMEM((N_Y, N_Z, PAD, BS), jnp.bfloat16),
            pltpu.VMEM((devices, BS), jnp.int32),
            pltpu.SMEM((devices, BS), jnp.int32),
            pltpu.SMEM((RG,), jnp.int32),
            pltpu.SemaphoreType.DMA((1,)),
        ],
        compiler_params=pltpu.CompilerParams(vmem_limit_bytes=2 * 2**20),
        cost_estimate=pl.CostEstimate(flops=0, bytes_accessed=2**20, transcendentals=0),
    )(rest)


def multiply_kernel(place, columns, spots, inner, left, rest, *refs):
    pieces, (out, held, strips, table, sem) = refs[:10], refs[10:]
    row = pl.program_id(0)

    @pl.when(row == 0)
    def load():
        copies = []
        slot = 0
        for i, piece in enumerate(pieces):
            blocks = piece.shape[0] // BS
            copies.append(
                pltpu.make_async_copy(
                    piece.at[pl.ds(0, blocks * BS)],
                    held.at[pl.ds(slot * BS, blocks * BS)],
                    sem.at[RG + i],
                )
            )
            slot += blocks
        for copy in copies:
            copy.start()
        held[pl.ds(N_RIGHT * BS, BS), :] = jnp.zeros((BS, BS), jnp.bfloat16)

        def list_row(n, carry):
            y, z = n // N_Z, n % N_Z
            d = z * N_Y + y
            for b in range(2):
                r, p = spots[2 * n + b] // PER_ROW, spots[2 * n + b] % PER_ROW
                column = pl.ds(pl.multiple_of(p * BS, BS), BS)
                rows = BS - REST * b
                pltpu.make_async_copy(
                    left.at[d, pl.ds(b * BS, rows), :], strips.at[r, pl.ds(0, rows), column], sem.at[r]
                ).start()
                if b:
                    pltpu.make_async_copy(
                        rest.at[y, z, pl.ds(0, REST), :], strips.at[r, pl.ds(rows, REST), column], sem.at[r]
                    ).start()
            return carry

        lax.fori_loop(0, N_LEFT // 2, list_row, 0, unroll=2)
        own_x, own_core = place[0] // 2, place[0] % 2

        def clear(i, carry):
            table[i] = N_RIGHT * BS
            return carry

        lax.fori_loop(0, KS * JB, clear, 0, unroll=16)

        def fill(k, carry):
            g, i = k // OWN_K, k % OWN_K
            s = ((g + own_core) % 2) * N_X + (g // 2 + N_X - own_x) % N_X
            for m in range(NBR):
                table[k * JB + columns[s, i * NBR + m]] = ((s * OWN_K + i) * NBR + m) * BS
            return carry

        lax.fori_loop(0, KS, fill, 0, unroll=2)
        for copy in copies:
            copy.wait()

    strip = strips.at[row]
    pltpu.make_async_copy(strip, strip, sem.at[row]).wait()
    ks = [inner[row * PER_ROW + p] for p in range(PER_ROW)]
    for j in range(0, JB, 2):
        rhs = jnp.concatenate(
            [
                jnp.concatenate(
                    [held[pl.ds(pl.multiple_of(table[k + j + h], BS), BS), :] for h in range(2)],
                    axis=1,
                )
                for k in ks
            ],
            axis=0,
        )
        out[:, j * BS : (j + 2) * BS] = jnp.dot(
            strip[...], rhs, preferred_element_type=jnp.float32
        ).astype(out.dtype)


def multiply(place, columns, lists, left, rest, pieces):
    hbm = pl.BlockSpec(memory_space=pl.ANY)
    return pl.pallas_call(
        multiply_kernel,
        grid=(RG,),
        out_shape=jax.ShapeDtypeStruct((RG * BS, JB * BS), jnp.bfloat16),
        in_specs=[pl.BlockSpec(memory_space=pltpu.SMEM)] * 4 + [hbm] * (2 + len(pieces)),
        out_specs=pl.BlockSpec((BS, JB * BS), lambda r: (r, 0)),
        scratch_shapes=[
            pltpu.VMEM(((N_RIGHT + 1) * BS, BS), jnp.bfloat16),
            pltpu.VMEM((RG, BS, PER_ROW * BS), jnp.bfloat16),
            pltpu.SMEM((KS * JB,), jnp.int32),
            pltpu.SemaphoreType.DMA((RG + len(pieces),)),
        ],
        compiler_params=pltpu.CompilerParams(vmem_limit_bytes=24 * 2**20),
        cost_estimate=pl.CostEstimate(flops=4 * 2**30, bytes_accessed=14 * 2**20, transcendentals=0),
    )(place, columns, *lists, *(pltpu.with_memory_space_constraint(v, pltpu.HBM) for v in [left, rest, *pieces]))


def tail(values):
    flat = values.astype(jnp.bfloat16).reshape(1, -1)
    return jnp.pad(flat, ((0, PAD - 1), (0, BS - flat.shape[1])))


def gather_right(own, first, second):
    after = lax.ppermute(own, "grp", shift_x(-1))
    before = lax.ppermute(own, "grp", shift_x(1))
    onward, back = lax.optimization_barrier((before, after, first))[:2]
    far_head = lax.ppermute(onward[: R_ROWS // 2], "grp", shift_x(1))
    far_tail = lax.ppermute(back[R_ROWS // 2 :], "grp", shift_x(-1))
    mine = [own, after, far_head, far_tail, before]
    far_head, far_tail = lax.optimization_barrier((far_head, far_tail, second))[:2]
    others = [own, after, far_head, far_tail, before]
    return mine + [lax.ppermute(v, "grp", SWAP_CORES) for v in others]


def spread(own, lines):
    copies = jnp.broadcast_to(own[None], (len(lines[0]),) + own.shape)
    return lax.all_to_all(copies, "col", 0, 0, axis_index_groups=lines)


def body(panel_blocks, panel_rows, panel_inner, right_blocks, right_columns):
    right = jnp.concatenate([right_blocks.reshape(R_ROWS, BS), tail(right_columns)])
    left = panel_blocks.reshape(L_ROWS, BS)
    line = spread(left[: L_ROWS - REST], Y_LINES)
    lefts = lax.all_gather(line, "col", axis=0, tiled=True, axis_index_groups=Z_LINES)
    rest = jnp.concatenate([left[L_ROWS - REST :], tail(jnp.concatenate([panel_rows, panel_inner]))])
    rest = lax.optimization_barrier((rest, line))[0]
    strip = spread(rest, Z_LINES)
    rest = spread(strip, Y_LINES)
    pieces = gather_right(right, strip, rest)
    place = lax.axis_index("grp").reshape(1)
    columns = read_columns(pieces)
    return multiply(place, columns, make_lists(rest), lefts, rest, pieces)


def solution(mesh):
    placed = (
        P(("grp", "col"), None, None),
        P(("grp", "col")),
        P(("grp", "col")),
        P("grp", "col", None, None),
        P("grp", "col"),
    )
    return jax.shard_map(
        body, mesh=mesh, in_specs=placed, out_specs=P("grp", "col"), check_vma=False
    )
```
